32 devices in a mesh: row: 16 (over z, y, x), col: 2 (over core).
Axes of the slice: x: 2, y: 2, z: 4, core: 2. Of those that a mesh axis runs over, the one named last changes fastest.
Arguments:
- traces: float32 [16, 8192], P('col', 'row'), may hold values from -50 to 50
Outputs:
- overwritten: float32 [8192, 4096], P('row', 'col')
- coupling: float32 [256, 4096], P(None, 'col')
The draws below stay inside these ranges and needn't reach their ends.
All inputs are finite; a program needn't handle non-finite values.
Results may differ from the reference program's by a relative error of at most 0.0015.
Values sent between devices are 32-bit elements; how exact they have to be, the bound alone decides.
No kernel may reach another device: no remote copies, remote signals or barrier semaphores. Data moves between devices by JAX's collectives and lax.ppermute only.
A program may use at most 64 MiB of HBM per device.

```python
import math
import jax
import jax.numpy as jnp
from jax import lax

CH = 16
TAPS = 256
ROWS = 8192
WIDE = 256


def draw_traces(key, part):
    subkeys = jax.random.split(key, 4)
    gains = jnp.exp(jax.random.uniform(subkeys[0], (CH, 1), jnp.float32, math.log(0.5), math.log(2.0)))
    roughness = jnp.exp(jax.random.uniform(subkeys[1], (CH, ROWS), jnp.float32, math.log(0.5), math.log(2.0)))
    timeline = jnp.arange(ROWS, dtype=jnp.float32) / ROWS
    envelope = 0.5 + timeline
    own_noise = jax.random.truncated_normal(subkeys[2], -5.0, 5.0, (CH, ROWS + 1), jnp.float32)
    common = jax.random.truncated_normal(subkeys[3], -5.0, 5.0, (1, ROWS), jnp.float32)
    shared = 0.6
    separate = 0.6
    filtered = own_noise[:, 1:] + 0.7 * own_noise[:, :-1]
    return gains * envelope[None, :] * roughness * (shared * common + separate * filtered)


def setup_inputs(seed: int = 0) -> dict:
    arg_keys = jax.random.split(jax.random.key(seed), 2)
    return {
        "traces": draw_traces(jax.random.fold_in(arg_keys[1], 71), 0),
    }


def trace_matrix(samples, offsets):
    padded = jnp.concatenate([jnp.zeros((TAPS,), jnp.float32), samples])
    return padded[offsets]

def reference(traces):
    highest = lax.Precision.HIGHEST
    offsets = (jnp.arange(ROWS)[:, None] - jnp.arange(TAPS)[None, :] + TAPS).astype(jnp.int32)
    panel_cols = trace_matrix(traces[0], offsets)[:, :WIDE]
    gram_sum = jnp.dot(panel_cols.T, panel_cols, precision=highest) / ROWS
    factor_low = jnp.linalg.cholesky(gram_sum)
    inverse = jax.scipy.linalg.solve_triangular(factor_low, jnp.eye(WIDE, dtype=jnp.float32), lower=True)
    basis_cols = jnp.dot(panel_cols, inverse.T, precision=highest)

    def one_trace(samples):
        blocked = trace_matrix(samples, offsets)
        coupled = jnp.dot(inverse, jnp.dot(panel_cols.T, blocked, precision=highest) / ROWS, precision=highest)
        return (coupled, blocked - jnp.dot(basis_cols, coupled, precision=highest))
    coupled, remainder = lax.map(one_trace, traces)
    coupling = jnp.transpose(coupled, (1, 0, 2)).reshape(WIDE, CH * TAPS)
    overwritten = jnp.transpose(remainder, (1, 0, 2)).reshape(ROWS, CH * TAPS)
    overwritten = overwritten.at[:, :WIDE].set(basis_cols)
    return (overwritten, coupling)
```

```python
import functools

import jax
import jax.numpy as jnp
from jax import lax
from jax.experimental import pallas as pl
from jax.experimental.pallas import tpu as pltpu
from jax.sharding import PartitionSpec as P

TAPS = 256
WIDE = 256
LANES = 128
PANEL = 32
F32 = jnp.float32
BF16 = jnp.bfloat16
LEFT = (0, 0, 1, 0, 2, 1)
RIGHT = (0, 1, 0, 2, 0, 1)
NT = (((1,), (1,)), ((), ()))
TN = (((0,), (0,)), ((), ()))


def split(x, count=3):
    pieces = []
    for _ in range(count - 1):
        pieces.append(x.astype(BF16))
        x = x - pieces[-1].astype(F32)
    pieces.append(x.astype(BF16))
    return pieces


def dot(a, b, dims=None):
    if dims is None:
        return jnp.dot(a, b, preferred_element_type=F32)
    return lax.dot_general(a, b, dims, preferred_element_type=F32)


def dot_split(a, b, dims=None):
    return dot(a[0], b[0], dims) + (dot(a[0], b[1], dims) + dot(a[1], b[0], dims))


def row_of(x, j):
    return jnp.broadcast_to(x[j : j + 1, :], x.shape)


def inverse_factor(m, n):
    sub = lax.broadcasted_iota(jnp.int32, (8, LANES), 0)
    groups = PANEL // 8
    half = n // LANES
    for r0 in range(0, n, PANEL):
        cols = list(range(r0 // LANES, half)) + [half + i for i in range((r0 + PANEL - 1) // LANES + 1)]
        v = [{c: m[r0 + 8 * g : r0 + 8 * g + 8, LANES * c : LANES * (c + 1)] for c in cols} for g in range(groups)]
        for p in range(groups):
            tile, lane = divmod(r0 + 8 * p, LANES)
            col = [
                [jnp.broadcast_to(v[g][tile][:, lane + k : lane + k + 1], (8, LANES)) if g >= p else None for g in range(groups)]
                for k in range(8)
            ]
            pivots = jnp.ones((8, LANES), F32)
            for j in range(8):
                pivot = row_of(col[j][p], j)
                pivots = jnp.where(sub == j, pivot, pivots)
                if j == 7 and p == groups - 1:
                    continue
                inv = 1.0 / pivot
                first = p if j < 7 else p + 1
                factor = {g: col[j][g] * inv for g in range(first, groups)}
                if first == p:
                    factor[p] = jnp.where(sub > j, factor[p], 0.0)
                for k in range(j + 1, 8):
                    row = row_of(col[k][p], j)
                    for g in range(first, groups):
                        col[k][g] = col[k][g] - factor[g] * row
                for c in cols:
                    row = row_of(v[p][c], j)
                    for g in range(first, groups):
                        v[g][c] = v[g][c] - factor[g] * row
            scale = lax.rsqrt(pivots)
            for c in cols:
                v[p][c] = v[p][c] * scale
        for g in range(groups):
            for c in cols:
                m[r0 + 8 * g : r0 + 8 * g + 8, LANES * c : LANES * (c + 1)] = v[g][c]
        done = r0 + PANEL
        if done < n:
            pieces = {c: split(jnp.concatenate([v[g][c] for g in range(groups)], 0)) for c in cols}
            for a in range(done // LANES, half):
                left = jnp.concatenate([pieces[a][i] for i in LEFT], 0)
                skip = max(0, done - LANES * a)
                for c in cols:
                    if c >= a:
                        right = jnp.concatenate([pieces[c][i] for i in RIGHT], 0)
                        update = dot(left, right, TN)
                        m[LANES * a + skip : LANES * (a + 1), LANES * c : LANES * (c + 1)] -= update[skip:, :]


def toeplitz(base, first, rows, store):
    width = base.shape[1]
    tiles = width // LANES
    strip = pltpu.roll(jnp.broadcast_to(base, (8, width)), first, 1, stride=1, stride_axis=0)
    for g in range(LANES // 8):
        turned = pltpu.roll(strip, 8 * g, 1) if g else strip
        for h in range(rows // LANES):
            for j in range(TAPS // LANES):
                t = (j - h) % tiles
                store(LANES * h + 8 * g, LANES * j, turned[:, LANES * t : LANES * (t + 1)])


def kernel(
    sizes, place, seen, over_out, coup_out,
    natural, lead, reverse_lead, lags, cross, gram, tail_low, tail_left, window, panel, over, coup, sems_a, sems_b,
):
    n_row, n_col, nc, rows = sizes
    per = rows // LANES
    blocks = n_row * per
    total = n_row * rows
    lag_tiles = TAPS // LANES
    my_row, my_col = place[0], place[1]

    for r in range(n_row):
        for q in range(per):
            t = r * per + q
            natural[t * nc : (t + 1) * nc, :] = seen[r * n_col + my_col, :, LANES * q : LANES * (q + 1)]
            lead[8 + t : 9 + t, :] = seen[r * n_col, 0:1, LANES * q : LANES * (q + 1)]
    lead[0:8, :] = jnp.zeros((8, LANES), F32)
    lead[8 + blocks : 16 + blocks, :] = jnp.zeros((8, LANES), F32)

    ia = lax.broadcasted_iota(jnp.int32, (LANES, LANES), 0)
    ib = lax.broadcasted_iota(jnp.int32, (LANES, LANES), 1)
    turn = (ia + ib == LANES - 1).astype(F32).astype(BF16)

    def samples(c):
        if c == nc:
            return lead[8 : 8 + blocks, :]
        return natural[pl.ds(c, blocks, stride=nc), :]

    step = lax.broadcasted_iota(jnp.int32, (blocks, LANES), 0)
    shifted = []
    for a in range(-lag_tiles, lag_tiles + 1):
        piece = lead[8 + a : 8 + a + blocks, :]
        keep = step < blocks - lag_tiles if a >= 0 else step + a < blocks - lag_tiles
        shifted.append(jnp.where(keep, piece, 0.0))
    right = split(jnp.concatenate(shifted, 1))
    right = jnp.concatenate([right[i] for i in RIGHT], 0)
    width = right.shape[1]
    for c in [nc] + list(range(nc)):
        pieces = split(samples(c))
        left = dot(turn, jnp.concatenate([pieces[i] for i in LEFT], 0), NT).astype(BF16)
        z = dot(left, right)
        parts = [z[8 * g : 8 * g + 8, :] for g in range(LANES // 8)]
        size = 8
        while len(parts) > 1:
            parts = [parts[i] + pltpu.roll(parts[i + 1], size, 1) for i in range(0, len(parts), 2)]
            size *= 2
        skewed = pltpu.roll(parts[0], 0, 1, stride=1, stride_axis=0)
        lags[c : c + 1, :] = jnp.sum(skewed, axis=0, keepdims=True)

    def put(ref, base):
        def store(i, j, tile):
            ref[i : i + 8, base + j : base + j + LANES] = tile

        return store

    zeros = jnp.zeros((1, TAPS), F32)

    def reversed_blocks(c, first, count):
        if c == nc:
            piece = lead[pl.ds(8 + first, count), :]
        else:
            piece = jnp.concatenate([natural[pl.ds((first + q) * nc + c, 1), :] for q in range(count)], 0)
        flipped = sum(dot(x, turn) for x in reversed(split(piece)))
        return jnp.concatenate([flipped[q : q + 1, :] for q in reversed(range(count))], 1)

    forward = jnp.concatenate([lead[8 + blocks - lag_tiles + q : 9 + blocks - lag_tiles + q, :] for q in range(lag_tiles)], 1)
    toeplitz(jnp.concatenate([forward, zeros], 1), 0, TAPS, put(tail_left, 0))
    left_pieces = split(tail_left[...])
    left6 = jnp.concatenate([left_pieces[i] for i in LEFT], 1)

    def crossed(c, out, base):
        toeplitz(jnp.concatenate([reversed_blocks(c, blocks - lag_tiles, lag_tiles), zeros], 1), 1 + TAPS, TAPS, put(tail_low, 0))
        toeplitz(lags[c : c + 1, :], 1 + TAPS, TAPS, put(out, base))
        pieces = split(tail_low[...])
        extra = dot(left6, jnp.concatenate([pieces[i] for i in RIGHT], 0))
        out[:, base : base + TAPS] = (out[:, base : base + TAPS] + extra) * (1.0 / total)

    crossed(nc, gram, 0)
    ga = lax.broadcasted_iota(jnp.int32, (WIDE, WIDE), 0)
    gb = lax.broadcasted_iota(jnp.int32, (WIDE, WIDE), 1)
    gram[:, WIDE:] = (ga == gb).astype(F32)
    inverse_factor(gram, WIDE)
    inverse = split(gram[:, WIDE:], 2)

    history = jnp.where(my_row > 0, 1.0, 0.0)
    start = my_row * per

    def own_rows(c, ref):
        now = reversed_blocks(c, start, per)
        before = reversed_blocks(c, jnp.maximum(start - lag_tiles, 0), lag_tiles) * history
        toeplitz(jnp.concatenate([now, before], 1), 1 + TAPS, rows, put(ref, 0))

    own_rows(nc, window)
    basis_all = dot_split(split(window[...], 2), inverse, NT)
    panel[...] = basis_all
    basis = split(basis_all, 2)

    copies = []
    for c in range(nc):
        at = pl.ds(c * TAPS, TAPS)
        crossed(c, cross, 0)
        coupling = dot_split(inverse, split(cross[...], 2))
        coup[:, at] = coupling
        copies.append(pltpu.make_async_copy(coup.at[:, at], coup_out.at[:, at], sems_a.at[c]))
        copies[-1].start()
        own_rows(c, window)
        rest = window[...] - dot_split(basis, split(coupling, 2))
        if c * TAPS < WIDE:
            rest = jnp.where(my_col == 0, panel[...], rest)
        over[:, at] = rest
        copies.append(pltpu.make_async_copy(over.at[:, at], over_out.at[:, at], sems_b.at[c]))
        copies[-1].start()
    for copy in copies:
        copy.wait()


def body(traces):
    n_row, n_col = lax.axis_size("row"), lax.axis_size("col")
    nc, rows = traces.shape
    sent = jnp.broadcast_to(traces[None], (n_row * n_col, nc, rows))
    seen = lax.all_to_all(sent, ("row", "col"), 0, 0)
    place = jnp.stack([lax.axis_index("row"), lax.axis_index("col")]).astype(jnp.int32)
    blocks = n_row * rows // LANES
    lag_tiles = TAPS // LANES
    return pl.pallas_call(
        functools.partial(kernel, (n_row, n_col, nc, rows)),
        out_shape=(
            jax.ShapeDtypeStruct((rows, nc * TAPS), F32),
            jax.ShapeDtypeStruct((WIDE, nc * TAPS), F32),
        ),
        in_specs=[pl.BlockSpec(memory_space=pltpu.SMEM), pl.BlockSpec(memory_space=pltpu.VMEM)],
        out_specs=[pl.BlockSpec(memory_space=pl.ANY)] * 2,
        scratch_shapes=[
            pltpu.VMEM((blocks * nc, LANES), F32),
            pltpu.VMEM((blocks + 16, LANES), F32),
            pltpu.VMEM((8, LANES), F32),
            pltpu.VMEM((nc + 8, (2 * lag_tiles + 1) * LANES), F32),
            pltpu.VMEM((WIDE, TAPS), F32),
            pltpu.VMEM((WIDE, 2 * WIDE), F32),
            pltpu.VMEM((TAPS, TAPS), F32),
            pltpu.VMEM((WIDE, TAPS), F32),
            pltpu.VMEM((rows, TAPS), F32),
            pltpu.VMEM((rows, WIDE), F32),
            pltpu.VMEM((rows, nc * TAPS), F32),
            pltpu.VMEM((WIDE, nc * TAPS), F32),
            pltpu.SemaphoreType.DMA((nc,)),
            pltpu.SemaphoreType.DMA((nc,)),
        ],
        compiler_params=pltpu.CompilerParams(vmem_limit_bytes=48 * 2**20),
    )(place, seen)


def solution(mesh):
    return jax.shard_map(
        body,
        mesh=mesh,
        in_specs=(P("col", "row"),),
        out_specs=(P("row", "col"), P(None, "col")),
        check_vma=False,
    )
```

```python
import functools

import jax
import jax.numpy as jnp
from jax import lax
from jax.experimental import pallas as pl
from jax.experimental.pallas import tpu as pltpu
from jax.sharding import PartitionSpec as P

TAPS = 256
WIDE = 256
LANES = 128
PANEL = 32
F32 = jnp.float32
BF16 = jnp.bfloat16
LEFT = (0, 0, 1, 0, 2, 1)
RIGHT = (0, 1, 0, 2, 0, 1)
SHORT = 3
NT = (((1,), (1,)), ((), ()))
TN = (((0,), (0,)), ((), ()))


def split(x, count=3):
    pieces = []
    for _ in range(count - 1):
        pieces.append(x.astype(BF16))
        x = x - pieces[-1].astype(F32)
    pieces.append(x.astype(BF16))
    return pieces


def dot(a, b, dims=None):
    if dims is None:
        return jnp.dot(a, b, preferred_element_type=F32)
    return lax.dot_general(a, b, dims, preferred_element_type=F32)


def joined(pieces, order, axis):
    return jnp.concatenate([pieces[i] for i in order], axis)


def row_of(x, j):
    return jnp.broadcast_to(x[j : j + 1, :], x.shape)


def inverse_factor(m, n):
    sub = lax.broadcasted_iota(jnp.int32, (8, LANES), 0)
    groups = PANEL // 8
    half = n // LANES
    for r0 in range(0, n, PANEL):
        cols = list(range(r0 // LANES, half)) + [half + i for i in range((r0 + PANEL - 1) // LANES + 1)]
        v = [{c: m[r0 + 8 * g : r0 + 8 * g + 8, LANES * c : LANES * (c + 1)] for c in cols} for g in range(groups)]
        for p in range(groups):
            tile, lane = divmod(r0 + 8 * p, LANES)
            col = [
                [jnp.broadcast_to(v[g][tile][:, lane + k : lane + k + 1], (8, LANES)) if g >= p else None for g in range(groups)]
                for k in range(8)
            ]
            pivots = jnp.ones((8, LANES), F32)
            for j in range(8):
                pivot = row_of(col[j][p], j)
                pivots = jnp.where(sub == j, pivot, pivots)
                if j == 7 and p == groups - 1:
                    continue
                inv = 1.0 / pivot
                first = p if j < 7 else p + 1
                factor = {g: col[j][g] * inv for g in range(first, groups)}
                if first == p:
                    factor[p] = jnp.where(sub > j, factor[p], 0.0)
                for k in range(j + 1, 8):
                    row = row_of(col[k][p], j)
                    for g in range(first, groups):
                        col[k][g] = col[k][g] - factor[g] * row
                for c in cols:
                    row = row_of(v[p][c], j)
                    for g in range(first, groups):
                        v[g][c] = v[g][c] - factor[g] * row
            scale = lax.rsqrt(pivots)
            for c in cols:
                v[p][c] = v[p][c] * scale
        for g in range(groups):
            for c in cols:
                m[r0 + 8 * g : r0 + 8 * g + 8, LANES * c : LANES * (c + 1)] = v[g][c]
        done = r0 + PANEL
        if done < n:
            pieces = {c: split(jnp.concatenate([v[g][c] for g in range(groups)], 0)) for c in cols}
            for a in range(done // LANES, half):
                left = jnp.concatenate([pieces[a][i] for i in LEFT], 0)
                skip = max(0, done - LANES * a)
                for c in cols:
                    if c >= a:
                        right = jnp.concatenate([pieces[c][i] for i in RIGHT], 0)
                        update = dot(left, right, TN)
                        m[LANES * a + skip : LANES * (a + 1), LANES * c : LANES * (c + 1)] -= update[skip:, :]


def strips(base, first):
    width = base.shape[1]
    strip = pltpu.roll(jnp.broadcast_to(base, (8, width)), first, 1, stride=1, stride_axis=0)
    return [pltpu.roll(strip, 8 * g, 1) if g else strip for g in range(LANES // 8)]


def tile_of(turned, block, lane):
    tiles = turned.shape[1] // LANES
    t = (lane - block) % tiles
    return turned[:, LANES * t : LANES * (t + 1)]


def expand(base, first, rows, ref, row, lane):
    for g, turned in enumerate(strips(base, first)):
        for h in range(rows // LANES):
            for j in range(TAPS // LANES):
                at = row + LANES * h + 8 * g
                ref[at : at + 8, lane + LANES * j : lane + LANES * (j + 1)] = tile_of(turned, h, j)


def expand_split(base, first, rows, refs, row, lane):
    turned = strips(base, first)
    for g in range(0, LANES // 8, 2):
        for h in range(rows // LANES):
            for j in range(TAPS // LANES):
                tile = jnp.concatenate([tile_of(turned[g], h, j), tile_of(turned[g + 1], h, j)], 0)
                at = row + LANES * h + 8 * g
                for ref, piece in zip(refs, split(tile, len(refs))):
                    ref[at : at + 16, lane + LANES * j : lane + LANES * (j + 1)] = piece


def turn_matrix():
    a = lax.broadcasted_iota(jnp.int32, (LANES, LANES), 0)
    b = lax.broadcasted_iota(jnp.int32, (LANES, LANES), 1)
    return (a + b == LANES - 1).astype(F32).astype(BF16)


def flip(x, turn):
    h, m, l = split(x)
    return dot(h, turn) + (dot(m, turn) + dot(l, turn))


def in_row(x, rows):
    return jnp.concatenate([x[r : r + 1, :] for r in rows], 1)


def read_lead(lead, first, n_row, n_col, per):
    blocks = n_row * per
    for r in range(n_row):
        for q in range(per):
            t = r * per + q
            lead[8 + t : 9 + t, :] = first[r * n_col, 0:1, LANES * q : LANES * (q + 1)]
    lead[0:8, :] = jnp.zeros((8, LANES), F32)
    lead[8 + blocks : 16 + blocks, :] = jnp.zeros((8, LANES), F32)


def shifted(lead, blocks, lowest, order):
    tail = TAPS // LANES
    step = lax.broadcasted_iota(jnp.int32, (blocks, LANES), 0)
    moved = []
    for a in range(lowest, tail + 1):
        keep = step < blocks - tail if a >= 0 else step + a < blocks - tail
        moved.append(jnp.where(keep, lead[8 + a : 8 + a + blocks, :], 0.0))
    return joined(split(jnp.concatenate(moved, 1)), order, 0)


def block_products(x, right, turn, order):
    left = dot(turn, joined(split(x), order, 0), NT).astype(BF16)
    return dot(left, right)


def skewed_sum(parts):
    size = 8
    while len(parts) > 1:
        parts = [parts[i] + pltpu.roll(parts[i + 1], size, 1) for i in range(0, len(parts), 2)]
        size *= 2
    rows = [pltpu.roll(parts[0][r : r + 8, :], 0, 1, stride=1, stride_axis=0) for r in range(0, parts[0].shape[0], 8)]
    return [jnp.sum(x, axis=0, keepdims=True) for x in rows]


def factor_kernel(sizes, place, first, factor_high, factor_low, basis_high, basis_low, lead, gram, window):
    n_row, n_col, nc, rows = sizes
    per = rows // LANES
    blocks = n_row * per
    tail = TAPS // LANES
    scale = 1.0 / (n_row * rows)
    read_lead(lead, first, n_row, n_col, per)
    turn = turn_matrix()
    zeros = jnp.zeros((1, TAPS), F32)

    last = lead[8 + blocks - tail : 8 + blocks, :]
    expand(jnp.concatenate([in_row(last, range(tail)), zeros], 1), 0, TAPS, window, 0, 0)
    left = joined(split(window[0:TAPS, :]), LEFT, 1)
    short_left = window[0:TAPS, :]
    expand(jnp.concatenate([in_row(flip(last, turn), reversed(range(tail))), zeros], 1), 1 + TAPS, TAPS, window, 0, 0)
    extra = dot(left, joined(split(window[0:TAPS, :]), RIGHT, 0))

    right = shifted(lead, blocks, -1, RIGHT)
    z = block_products(lead[8 : 8 + blocks, :], right, turn, LEFT)
    lags = skewed_sum([z[r : r + 8, :] for r in range(0, LANES, 8)])[0]
    expand(lags, 1 + TAPS, WIDE, gram, 0, 0)
    gram[:, 0:WIDE] = (gram[:, 0:WIDE] + extra) * scale
    a = lax.broadcasted_iota(jnp.int32, (WIDE, WIDE), 0)
    b = lax.broadcasted_iota(jnp.int32, (WIDE, WIDE), 1)
    gram[:, WIDE:] = (a == b).astype(F32)
    inverse_factor(gram, WIDE)

    inverse = gram[:, WIDE:]
    pieces = split(inverse, 2)
    scaled = split(inverse * scale, 2)
    fold = split(dot(joined(scaled, LEFT[:SHORT], 1), joined(split(short_left, 2), RIGHT[:SHORT], 0)), 2)
    for ref, a, b in ((factor_high, scaled[0], fold[0]), (factor_low, scaled[1], fold[1])):
        ref[:, 0:WIDE] = a
        ref[:, WIDE:] = b

    start = place[0] * per
    own = flip(lead[pl.ds(8 + start - tail, per + tail), :], turn)
    expand(in_row(own, reversed(range(per + tail))), 1 + TAPS, rows, window, 0, 0)
    basis = dot(joined(split(window[...], 2), LEFT[:SHORT], 1), joined(pieces, RIGHT[:SHORT], 1), NT)
    basis_high[...], basis_low[...] = split(basis, 2)


def update_kernel(
    sizes, place, first, seen, factor_high, factor_low, basis_high, basis_low, over_out, coup_out,
    natural, lead, products, right_high, right_low, over, coup, over_sems, coup_sems,
):
    n_row, n_col, nc, rows = sizes
    per = rows // LANES
    blocks = n_row * per
    tail = TAPS // LANES
    turn = turn_matrix()
    zeros = jnp.zeros((1, TAPS), F32)
    read_lead(lead, first, n_row, n_col, per)
    for r in range(n_row):
        for q in range(per):
            t = r * per + q
            natural[t * nc : (t + 1) * nc, :] = seen[r, :, LANES * q : LANES * (q + 1)]

    start = place[0] * per
    rows_of = lambda t: natural[pl.ds(pl.multiple_of(t * nc, nc), nc), :]
    history = jnp.where(place[0] > 0, 1.0, 0.0)
    near = [rows_of(jnp.maximum(start + q, 0)) * (history if q < 0 else 1.0) for q in range(-tail, per)]
    near += [rows_of(blocks - tail + q) for q in range(tail)]
    near = flip(jnp.concatenate(near, 0), turn)

    right = shifted(lead, blocks, -tail, (0, 1, 0, 1))
    left = [joined(split(natural[pl.ds(c, blocks, stride=nc), :], 2), (0, 0, 1, 1), 0) for c in range(nc)]
    left = dot(turn, jnp.concatenate(left, 0), NT).astype(BF16)
    for c in range(nc):
        products[c] = dot(left[:, 4 * blocks * c : 4 * blocks * (c + 1)], right)
    parts = [products[:, r : r + 8, :].reshape(nc * 8, products.shape[2]) for r in range(0, LANES, 8)]
    lags = skewed_sum(parts)
    for c in range(nc):
        expand_split(lags[c], 1 + TAPS, TAPS, (right_high.at[c], right_low.at[c]), 0, 0)
        last = [(per + tail + q) * nc + c for q in reversed(range(tail))]
        expand_split(
            jnp.concatenate([in_row(near, last), zeros], 1), 1 + TAPS, TAPS, (right_high.at[c], right_low.at[c]), TAPS, 0
        )
    factor = jnp.concatenate([factor_high[...], factor_high[...], factor_low[...]], 1)
    basis = jnp.concatenate([basis_high[...], basis_high[...], basis_low[...]], 1)
    copies = []

    def couple(c):
        at = slice(c * TAPS, (c + 1) * TAPS)
        coupling = dot(factor, joined((right_high[c], right_low[c]), RIGHT[:SHORT], 0))
        coup[:, at] = coupling
        copies.append(pltpu.make_async_copy(coup.at[:, at], coup_out.at[:, at], coup_sems.at[c]))
        copies[-1].start()
        expand(in_row(near, [q * nc + c for q in reversed(range(per + tail))]), 1 + TAPS, rows, over, 0, c * TAPS)
        return joined(split(coupling, 2), RIGHT[:SHORT], 0)

    ahead = couple(0)
    for c in range(nc):
        at = slice(c * TAPS, (c + 1) * TAPS)
        now = ahead
        if c + 1 < nc:
            ahead = couple(c + 1)
        rest = over[:, at] - dot(basis, now)
        if c * TAPS < WIDE:
            rest = jnp.where(place[1] == 0, basis_high[...].astype(F32) + basis_low[...].astype(F32), rest)
        over[:, at] = rest
        copies.append(pltpu.make_async_copy(over.at[:, at], over_out.at[:, at], over_sems.at[c]))
        copies[-1].start()
    for copy in copies:
        copy.wait()


def factor_call(sizes, place, first):
    n_row, n_col, nc, rows = sizes
    blocks = n_row * rows // LANES
    small = jax.ShapeDtypeStruct((WIDE, WIDE + TAPS), BF16)
    tall = jax.ShapeDtypeStruct((rows, WIDE), BF16)
    return pl.pallas_call(
        functools.partial(factor_kernel, sizes),
        out_shape=(small, small, tall, tall),
        in_specs=[pl.BlockSpec(memory_space=pltpu.SMEM), pl.BlockSpec(memory_space=pltpu.VMEM)],
        out_specs=[pl.BlockSpec(memory_space=pltpu.VMEM)] * 4,
        scratch_shapes=[
            pltpu.VMEM((blocks + 16, LANES), F32),
            pltpu.VMEM((WIDE, 2 * WIDE), F32),
            pltpu.VMEM((max(rows, TAPS), TAPS), F32),
        ],
        compiler_params=pltpu.CompilerParams(vmem_limit_bytes=16 * 2**20),
        cost_estimate=pl.CostEstimate(flops=10**10, bytes_accessed=10**6, transcendentals=0),
    )(place, first)


def update_call(sizes, place, first, seen, parts):
    n_row, n_col, nc, rows = sizes
    blocks = n_row * rows // LANES
    return pl.pallas_call(
        functools.partial(update_kernel, sizes),
        out_shape=(
            jax.ShapeDtypeStruct((rows, nc * TAPS), F32),
            jax.ShapeDtypeStruct((WIDE, nc * TAPS), F32),
        ),
        in_specs=[pl.BlockSpec(memory_space=pltpu.SMEM)] + [pl.BlockSpec(memory_space=pltpu.VMEM)] * 6,
        out_specs=[pl.BlockSpec(memory_space=pl.ANY)] * 2,
        scratch_shapes=[
            pltpu.VMEM((blocks * nc, LANES), F32),
            pltpu.VMEM((blocks + 16, LANES), F32),
            pltpu.VMEM((nc, LANES, 2 * TAPS + LANES), F32),
            pltpu.VMEM((nc, 2 * TAPS, TAPS), BF16),
            pltpu.VMEM((nc, 2 * TAPS, TAPS), BF16),
            pltpu.VMEM((rows, nc * TAPS), F32),
            pltpu.VMEM((WIDE, nc * TAPS), F32),
            pltpu.SemaphoreType.DMA((nc,)),
            pltpu.SemaphoreType.DMA((nc,)),
        ],
        compiler_params=pltpu.CompilerParams(vmem_limit_bytes=40 * 2**20),
        cost_estimate=pl.CostEstimate(flops=10**10, bytes_accessed=10**7, transcendentals=0),
    )(place, first, seen, *parts)


def body(traces):
    n_row, n_col = lax.axis_size("row"), lax.axis_size("col")
    nc, rows = traces.shape
    sizes = (n_row, n_col, nc, rows)
    first = lax.all_to_all(jnp.broadcast_to(traces[None, 0:1], (n_row * n_col, 1, rows)), ("row", "col"), 0, 0)
    seen = lax.all_to_all(jnp.broadcast_to(traces[None], (n_row, nc, rows)), "row", 0, 0)
    place = jnp.stack([lax.axis_index("row"), lax.axis_index("col")]).astype(jnp.int32)
    parts = factor_call(sizes, place, first)
    return update_call(sizes, place, first, seen, parts)


def solution(mesh):
    return jax.shard_map(
        body,
        mesh=mesh,
        in_specs=(P("col", "row"),),
        out_specs=(P("row", "col"), P(None, "col")),
        check_vma=False,
    )
```

```python
import functools

import jax
import jax.numpy as jnp
from jax import lax
from jax.experimental import pallas as pl
from jax.experimental.pallas import tpu as pltpu
from jax.sharding import PartitionSpec as P

TAPS = 256
WIDE = 256
LANES = 128
PANEL = 32
SPAN = 16
FIRST = True
F32 = jnp.float32
BF16 = jnp.bfloat16
LEFT = (0, 0, 1, 0, 2, 1)
RIGHT = (0, 1, 0, 2, 0, 1)
SHORT = 3
NT = (((1,), (1,)), ((), ()))
TN = (((0,), (0,)), ((), ()))


def split(x, count=3):
    pieces = []
    for _ in range(count - 1):
        pieces.append(x.astype(BF16))
        x = x - pieces[-1].astype(F32)
    pieces.append(x.astype(BF16))
    return pieces


def dot(a, b, dims=None):
    if dims is None:
        return jnp.dot(a, b, preferred_element_type=F32)
    return lax.dot_general(a, b, dims, preferred_element_type=F32)


def joined(pieces, order, axis):
    return jnp.concatenate([pieces[i] for i in order], axis)


def row_of(x, j):
    return jnp.broadcast_to(x[j : j + 1, :], x.shape)


def inverse_factor(m, n, pause):
    sub = lax.broadcasted_iota(jnp.int32, (8, LANES), 0)
    odd = sub % 2 == 1
    groups = PANEL // 8
    half = n // LANES
    for r0 in range(0, n, PANEL):
        tiles = list(range(r0 // LANES, half)) + [half + i for i in range((r0 + PANEL - 1) // LANES + 1)]
        v = [{c: m[r0 + 8 * g : r0 + 8 * g + 8, LANES * c : LANES * (c + 1)] for c in tiles} for g in range(groups)]
        pivots = [None] * groups
        for s in range(0, groups, SPAN // 8):
            col = [[None] * groups for _ in range(SPAN)]
            for k in range(SPAN):
                tile, lane = divmod(r0 + 8 * s + k, LANES)
                for g in range(s + k // 8, groups):
                    col[k][g] = jnp.broadcast_to(v[g][tile][:, lane : lane + 1], (8, LANES))
            for j in range(0, SPAN, 2):
                p, i = s + j // 8, j % 8
                x, y = col[j], col[j + 1]
                pivot = [row_of(x[p], i), row_of(x[p], i + 1), row_of(y[p], i + 1)]
                pivots[p] = pivot if i == 0 else [jnp.where(sub < i, old, new) for old, new in zip(pivots[p], pivot)]
                first = p if i < 6 else p + 1
                if first == groups:
                    continue
                a, b, c = pivot
                inv = 1.0 / (a * c - b * b)
                a, b, c = a * inv, b * inv, c * inv
                fx, fy = {}, {}
                for g in range(first, groups):
                    fx[g] = x[g] * c - y[g] * b
                    fy[g] = y[g] * a - x[g] * b
                    if g == p:
                        fx[g] = jnp.where(sub > i + 1, fx[g], 0.0)
                        fy[g] = jnp.where(sub > i + 1, fy[g], 0.0)
                for k in range(j + 2, SPAN):
                    gk = s + k // 8
                    rx, ry = row_of(x[gk], k % 8), row_of(y[gk], k % 8)
                    for g in range(gk, groups):
                        col[k][g] = col[k][g] - (fx[g] * rx + fy[g] * ry)
                for t in tiles:
                    rx, ry = row_of(v[p][t], i), row_of(v[p][t], i + 1)
                    for g in range(first, groups):
                        v[g][t] = v[g][t] - (fx[g] * rx + fy[g] * ry)
        for g in range(groups):
            a, b, c = pivots[g]
            ratio = b / a
            scale = lax.rsqrt(jnp.where(odd, c - b * ratio, a))
            ratio = jnp.where(odd, ratio, 0.0)
            for t in tiles:
                v[g][t] = (v[g][t] - ratio * pltpu.roll(v[g][t], 1, 0)) * scale
                m[r0 + 8 * g : r0 + 8 * g + 8, LANES * t : LANES * (t + 1)] = v[g][t]
        done = r0 + PANEL
        if done < n:
            pieces = {c: split(jnp.concatenate([v[g][c] for g in range(groups)], 0)) for c in tiles}
            right = {c: joined(pieces[c], RIGHT, 0) for c in tiles}
            updates = []
            for a in range(done // LANES, half):
                left = joined(pieces[a], LEFT, 0)
                updates += [(a, c, dot(left, right[c], TN)) for c in tiles if c >= a]
            pause()
            for a, c, update in updates:
                skip = max(0, done - LANES * a)
                m[LANES * a + skip : LANES * (a + 1), LANES * c : LANES * (c + 1)] -= update[skip:, :]


def shifted_rows(base, first, rows, step):
    strip = pltpu.roll(jnp.broadcast_to(base, (rows, base.shape[1])), first, 1, stride=1, stride_axis=0)
    return [strip[r : r + step, :] for r in range(0, rows, step)]


def tile_of(turned, block, lane):
    tiles = turned.shape[1] // LANES
    t = (lane - block) % tiles
    return turned[:, LANES * t : LANES * (t + 1)]


def expand(base, first, rows, ref, row, lane):
    for g, turned in enumerate(shifted_rows(base, first, LANES, 8)):
        for h in range(rows // LANES):
            for j in range(TAPS // LANES):
                at = row + LANES * h + 8 * g
                ref[at : at + 8, lane + LANES * j : lane + LANES * (j + 1)] = tile_of(turned, h, j)


def expand_split(base, first, rows, refs):
    (strip,) = shifted_rows(base, first, 16, 16)
    for ref, piece in zip(refs, split(strip, len(refs))):
        for g in range(0, LANES // 16):
            turned = pltpu.roll(piece, 16 * g, 1) if g else piece
            for h in range(rows // LANES):
                for j in range(TAPS // LANES):
                    at = LANES * h + 16 * g
                    ref[at : at + 16, LANES * j : LANES * (j + 1)] = tile_of(turned, h, j)


def run(steps):
    for _ in steps:
        pass


def turn_matrix():
    a = lax.broadcasted_iota(jnp.int32, (LANES, LANES), 0)
    b = lax.broadcasted_iota(jnp.int32, (LANES, LANES), 1)
    return (a + b == LANES - 1).astype(F32).astype(BF16)


def flip(x, turn):
    h, m, l = split(x)
    return dot(h, turn) + (dot(m, turn) + dot(l, turn))


def in_row(x, rows):
    return jnp.concatenate([x[r : r + 1, :] for r in rows], 1)


def read_lead(lead, seen, other, my_col, n_row, per):
    blocks = n_row * per
    here = my_col == 0
    for r in range(n_row):
        for q in range(per):
            t = r * per + q
            at = slice(LANES * q, LANES * (q + 1))
            lead[8 + t : 9 + t, :] = jnp.where(here, seen[r, 0:1, at], other[r, 0:1, at])
    lead[0:8, :] = jnp.zeros((8, LANES), F32)
    lead[8 + blocks : 16 + blocks, :] = jnp.zeros((8, LANES), F32)


def shifted(lead, blocks, lowest, order):
    tail = TAPS // LANES
    step = lax.broadcasted_iota(jnp.int32, (blocks, LANES), 0)
    moved = []
    for a in range(lowest, tail + 1):
        keep = step < blocks - tail if a >= 0 else step + a < blocks - tail
        moved.append(jnp.where(keep, lead[8 + a : 8 + a + blocks, :], 0.0))
    return joined(split(jnp.concatenate(moved, 1)), order, 0)


def block_products(x, right, turn, order):
    left = dot(turn, joined(split(x), order, 0), NT).astype(BF16)
    return dot(left, right)


def skewed_sum(z):
    return jnp.sum(pltpu.roll(z, 0, 1, stride=1, stride_axis=0), axis=0, keepdims=True)


def kernel(
    sizes, other, seen, over_out, coup_out,
    natural, lead, gram, window, products, low_high, low_low, cross, cross_high, cross_low, over, coup, over_sems, coup_sems,
):
    n_row, n_col, nc, rows = sizes
    per = rows // LANES
    blocks = n_row * per
    tail = TAPS // LANES
    scale = 1.0 / (n_row * rows)
    my_row, my_col = lax.axis_index("row"), lax.axis_index("col")
    start = my_row * per
    turn = turn_matrix()
    zeros = jnp.zeros((1, TAPS), F32)
    read_lead(lead, seen, other, my_col, n_row, per)

    z = block_products(lead[8 : 8 + blocks, :], shifted(lead, blocks, -1, RIGHT), turn, LEFT)
    lags = skewed_sum(z)

    last = lead[8 + blocks - tail : 8 + blocks, :]
    expand(jnp.concatenate([in_row(last, range(tail)), zeros], 1), 0, TAPS, window, 0, 0)
    left = split(window[0:TAPS, :])
    tail_left = joined(left, LEFT[:SHORT], 1)
    expand(jnp.concatenate([in_row(flip(last, turn), reversed(range(tail))), zeros], 1), 1 + TAPS, TAPS, gram, 0, WIDE)
    extra = dot(joined(left, LEFT, 1), joined(split(gram[:, WIDE:]), RIGHT, 0))

    expand(lags, 1 + TAPS, WIDE, gram, 0, 0)
    gram[:, 0:WIDE] = (gram[:, 0:WIDE] + extra) * scale
    a = lax.broadcasted_iota(jnp.int32, (WIDE, WIDE), 0)
    b = lax.broadcasted_iota(jnp.int32, (WIDE, WIDE), 1)
    gram[:, WIDE:] = (a == b).astype(F32)

    for r in range(n_row):
        for q in range(per):
            t = r * per + q
            natural[t * nc : (t + 1) * nc, :] = seen[r, :, LANES * q : LANES * (q + 1)]
    rows_of = lambda t: natural[pl.ds(pl.multiple_of(t * nc, nc), nc), :]
    history = jnp.where(my_row > 0, 1.0, 0.0)
    near = [rows_of(jnp.maximum(start + q, 0)) * (history if q < 0 else 1.0) for q in range(-tail, per)]
    near += [rows_of(blocks - tail + q) for q in range(tail)]
    near = flip(jnp.concatenate(near, 0), turn)
    own = flip(lead[pl.ds(8 + start - tail, per + tail), :], turn)
    expand(in_row(own, reversed(range(per + tail))), 1 + TAPS, rows, window, 0, 0)
    own_rows = joined(split(window[0:rows, :], 2), LEFT[:SHORT], 1)
    right = shifted(lead, blocks, -tail, (0, 1, 0, 1))
    left = [joined(split(natural[pl.ds(c, blocks, stride=nc), :], 2), (0, 0, 1, 1), 0) for c in range(nc)]
    left = dot(turn, jnp.concatenate(left, 0), NT).astype(BF16)

    def steps():
        for c in range(nc):
            products[c] = dot(left[:, 4 * blocks * c : 4 * blocks * (c + 1)], right)
        for c in range(nc):
            last = [(per + tail + q) * nc + c for q in reversed(range(tail))]
            refs = (low_high.at[c], low_low.at[c])
            expand_split(jnp.concatenate([in_row(near, last), zeros], 1), 1 + TAPS, TAPS, refs)
        yield
        for c in range(nc):
            expand(skewed_sum(products[c]), 1 + TAPS, TAPS, cross, 0, c * TAPS)
            if c % 2 == 1:
                yield
        for c in range(nc):
            at = slice(c * TAPS, (c + 1) * TAPS)
            whole = cross[:, at] + dot(tail_left, joined((low_high[c], low_low[c]), RIGHT[:SHORT], 0))
            cross_high[c], cross_low[c] = split(whole * scale, 2)
            if c % 4 == 3:
                yield

    rest = steps()
    if FIRST:
        run(rest)
    inverse_factor(gram, WIDE, lambda: next(rest, None))
    run(rest)

    pieces = split(gram[:, WIDE:], 2)
    factor = joined(pieces, LEFT[:SHORT], 1)
    panel = dot(own_rows, joined(pieces, RIGHT[:SHORT], 1), NT)
    basis = joined(split(panel, 2), LEFT[:SHORT], 1)
    copies = []

    def couple(c):
        at = slice(c * TAPS, (c + 1) * TAPS)
        coupling = dot(factor, joined((cross_high[c], cross_low[c]), RIGHT[:SHORT], 0))
        coup[:, at] = coupling
        copies.append(pltpu.make_async_copy(coup.at[:, at], coup_out.at[:, at], coup_sems.at[c]))
        copies[-1].start()
        expand(in_row(near, [q * nc + c for q in reversed(range(per + tail))]), 1 + TAPS, rows, over, 0, c * TAPS)
        return joined(split(coupling, 2), RIGHT[:SHORT], 0)

    ahead = couple(0)
    for c in range(nc):
        at = slice(c * TAPS, (c + 1) * TAPS)
        now = ahead
        if c + 1 < nc:
            ahead = couple(c + 1)
        rest = over[:, at] - dot(basis, now)
        if c * TAPS < WIDE:
            rest = jnp.where(my_col == 0, panel, rest)
        over[:, at] = rest
        copies.append(pltpu.make_async_copy(over.at[:, at], over_out.at[:, at], over_sems.at[c]))
        copies[-1].start()
    for copy in copies:
        copy.wait()


def call(sizes, other, seen):
    n_row, n_col, nc, rows = sizes
    blocks = n_row * rows // LANES
    return pl.pallas_call(
        functools.partial(kernel, sizes),
        out_shape=(
            jax.ShapeDtypeStruct((rows, nc * TAPS), F32),
            jax.ShapeDtypeStruct((WIDE, nc * TAPS), F32),
        ),
        in_specs=[pl.BlockSpec(memory_space=pltpu.VMEM)] * 2,
        out_specs=[pl.BlockSpec(memory_space=pl.ANY)] * 2,
        scratch_shapes=[
            pltpu.VMEM((blocks * nc, LANES), F32),
            pltpu.VMEM((blocks + 16, LANES), F32),
            pltpu.VMEM((WIDE, 2 * WIDE), F32),
            pltpu.VMEM((max(rows, TAPS), TAPS), F32),
            pltpu.VMEM((nc, LANES, 2 * TAPS + LANES), F32),
            pltpu.VMEM((nc, TAPS, TAPS), BF16),
            pltpu.VMEM((nc, TAPS, TAPS), BF16),
            pltpu.VMEM((WIDE, nc * TAPS), F32),
            pltpu.VMEM((nc, TAPS, TAPS), BF16),
            pltpu.VMEM((nc, TAPS, TAPS), BF16),
            pltpu.VMEM((rows, nc * TAPS), F32),
            pltpu.VMEM((WIDE, nc * TAPS), F32),
            pltpu.SemaphoreType.DMA((nc,)),
            pltpu.SemaphoreType.DMA((nc,)),
        ],
        compiler_params=pltpu.CompilerParams(vmem_limit_bytes=24 * 2**20),
    )(other, seen)


def body(traces):
    n_row, n_col = lax.axis_size("row"), lax.axis_size("col")
    nc, rows = traces.shape
    seen = lax.all_to_all(jnp.broadcast_to(traces[None], (n_row, nc, rows)), "row", 0, 0)
    col = lax.axis_index("col")
    first, step = seen[:, 0:1], 1
    while step < n_col:
        other = lax.ppermute(first, "col", [(i, i + step) for i in range(min(step, n_col - step))])
        first, step = jnp.where(col < step, first, other), 2 * step
    return call((n_row, n_col, nc, rows), other, seen)


def solution(mesh):
    return jax.shard_map(
        body,
        mesh=mesh,
        in_specs=(P("col", "row"),),
        out_specs=(P("row", "col"), P(None, "col")),
        check_vma=False,
    )
```

```python
import functools

import jax
import jax.numpy as jnp
from jax import lax
from jax.experimental import pallas as pl
from jax.experimental.pallas import tpu as pltpu
from jax.sharding import PartitionSpec as P

TAPS = 256
WIDE = 256
LANES = 128
PANEL = 32
SPAN = 16
FIRST = False
T = 0
S = 2
Q = 0
F32 = jnp.float32
BF16 = jnp.bfloat16
LEFT = (0, 0, 1, 0, 2, 1)
RIGHT = (0, 1, 0, 2, 0, 1)
SHORT = 3
NT = (((1,), (1,)), ((), ()))
TN = (((0,), (0,)), ((), ()))


def split(x, count=3):
    pieces = []
    for _ in range(count - 1):
        pieces.append(x.astype(BF16))
        x = x - pieces[-1].astype(F32)
    pieces.append(x.astype(BF16))
    return pieces


def dot(a, b, dims=None):
    if dims is None:
        return jnp.dot(a, b, preferred_element_type=F32)
    return lax.dot_general(a, b, dims, preferred_element_type=F32)


def joined(pieces, order, axis):
    return jnp.concatenate([pieces[i] for i in order], axis)


def row_of(x, j):
    return jnp.broadcast_to(x[j : j + 1, :], x.shape)


def inverse_factor(m, n, pause):
    sub = lax.broadcasted_iota(jnp.int32, (8, LANES), 0)
    odd = sub % 2 == 1
    groups = PANEL // 8
    half = n // LANES
    for r0 in range(0, n, PANEL):
        tiles = list(range(r0 // LANES, half)) + [half + i for i in range((r0 + PANEL - 1) // LANES + 1)]
        v = [{c: m[r0 + 8 * g : r0 + 8 * g + 8, LANES * c : LANES * (c + 1)] for c in tiles} for g in range(groups)]
        pivots = [None] * groups
        for s in range(0, groups, SPAN // 8):
            pause(S)
            col = [[None] * groups for _ in range(SPAN)]
            for k in range(SPAN):
                tile, lane = divmod(r0 + 8 * s + k, LANES)
                for g in range(s + k // 8, groups):
                    col[k][g] = jnp.broadcast_to(v[g][tile][:, lane : lane + 1], (8, LANES))
            for j in range(0, SPAN, 2):
                if j % 8 == 4:
                    pause(Q)
                p, i = s + j // 8, j % 8
                x, y = col[j], col[j + 1]
                pivot = [row_of(x[p], i), row_of(x[p], i + 1), row_of(y[p], i + 1)]
                pivots[p] = pivot if i == 0 else [jnp.where(sub < i, old, new) for old, new in zip(pivots[p], pivot)]
                first = p if i < 6 else p + 1
                if first == groups:
                    continue
                a, b, c = pivot
                inv = 1.0 / (a * c - b * b)
                a, b, c = a * inv, b * inv, c * inv
                fx, fy = {}, {}
                for g in range(first, groups):
                    fx[g] = x[g] * c - y[g] * b
                    fy[g] = y[g] * a - x[g] * b
                    if g == p:
                        fx[g] = jnp.where(sub > i + 1, fx[g], 0.0)
                        fy[g] = jnp.where(sub > i + 1, fy[g], 0.0)
                for k in range(j + 2, SPAN):
                    gk = s + k // 8
                    rx, ry = row_of(x[gk], k % 8), row_of(y[gk], k % 8)
                    for g in range(gk, groups):
                        col[k][g] = col[k][g] - (fx[g] * rx + fy[g] * ry)
                for t in tiles:
                    rx, ry = row_of(v[p][t], i), row_of(v[p][t], i + 1)
                    for g in range(first, groups):
                        v[g][t] = v[g][t] - (fx[g] * rx + fy[g] * ry)
        for g in range(groups):
            a, b, c = pivots[g]
            ratio = b / a
            scale = lax.rsqrt(jnp.where(odd, c - b * ratio, a))
            ratio = jnp.where(odd, ratio, 0.0)
            for t in tiles:
                v[g][t] = (v[g][t] - ratio * pltpu.roll(v[g][t], 1, 0)) * scale
                m[r0 + 8 * g : r0 + 8 * g + 8, LANES * t : LANES * (t + 1)] = v[g][t]
        done = r0 + PANEL
        if done < n:
            pieces = {c: split(jnp.concatenate([v[g][c] for g in range(groups)], 0)) for c in tiles}
            right = {c: joined(pieces[c], RIGHT, 0) for c in tiles}
            updates = []
            for a in range(done // LANES, half):
                left = joined(pieces[a], LEFT, 0)
                updates += [(a, c, dot(left, right[c], TN)) for c in tiles if c >= a]
            pause(T)
            for a, c, update in updates:
                skip = max(0, done - LANES * a)
                m[LANES * a + skip : LANES * (a + 1), LANES * c : LANES * (c + 1)] -= update[skip:, :]


def shifted_rows(base, first, rows, step):
    strip = pltpu.roll(jnp.broadcast_to(base, (rows, base.shape[1])), first, 1, stride=1, stride_axis=0)
    return [strip[r : r + step, :] for r in range(0, rows, step)]


def tile_of(turned, block, lane):
    tiles = turned.shape[1] // LANES
    t = (lane - block) % tiles
    return turned[:, LANES * t : LANES * (t + 1)]


def expand(base, first, rows, ref, row, lane):
    for g, turned in enumerate(shifted_rows(base, first, LANES, 8)):
        for h in range(rows // LANES):
            for j in range(TAPS // LANES):
                at = row + LANES * h + 8 * g
                ref[at : at + 8, lane + LANES * j : lane + LANES * (j + 1)] = tile_of(turned, h, j)


def expand_split(base, first, rows, refs):
    (strip,) = shifted_rows(base, first, 16, 16)
    for ref, piece in zip(refs, split(strip, len(refs))):
        for g in range(0, LANES // 16):
            turned = pltpu.roll(piece, 16 * g, 1) if g else piece
            for h in range(rows // LANES):
                for j in range(TAPS // LANES):
                    at = LANES * h + 16 * g
                    ref[at : at + 16, LANES * j : LANES * (j + 1)] = tile_of(turned, h, j)


def run(steps):
    for _ in steps:
        pass


def turn_matrix():
    a = lax.broadcasted_iota(jnp.int32, (LANES, LANES), 0)
    b = lax.broadcasted_iota(jnp.int32, (LANES, LANES), 1)
    return (a + b == LANES - 1).astype(F32).astype(BF16)


def flip(x, turn):
    h, m, l = split(x)
    return dot(h, turn) + (dot(m, turn) + dot(l, turn))


def in_row(x, rows):
    return jnp.concatenate([x[r : r + 1, :] for r in rows], 1)


def read_lead(lead, seen, other, my_col, n_row, per):
    blocks = n_row * per
    here = my_col == 0
    for r in range(n_row):
        for q in range(per):
            t = r * per + q
            at = slice(LANES * q, LANES * (q + 1))
            lead[8 + t : 9 + t, :] = jnp.where(here, seen[r, 0:1, at], other[r, 0:1, at])
    lead[0:8, :] = jnp.zeros((8, LANES), F32)
    lead[8 + blocks : 16 + blocks, :] = jnp.zeros((8, LANES), F32)


def shifted(lead, blocks, lowest, order):
    tail = TAPS // LANES
    step = lax.broadcasted_iota(jnp.int32, (blocks, LANES), 0)
    moved = []
    for a in range(lowest, tail + 1):
        keep = step < blocks - tail if a >= 0 else step + a < blocks - tail
        moved.append(jnp.where(keep, lead[8 + a : 8 + a + blocks, :], 0.0))
    return joined(split(jnp.concatenate(moved, 1)), order, 0)


def block_products(x, right, turn, order):
    left = dot(turn, joined(split(x), order, 0), NT).astype(BF16)
    return dot(left, right)


def skewed_sum(z):
    return jnp.sum(pltpu.roll(z, 0, 1, stride=1, stride_axis=0), axis=0, keepdims=True)


def kernel(
    sizes, other, seen, over_out, coup_out,
    natural, lead, gram, window, products, low_high, low_low, cross, cross_high, cross_low, over, coup, over_sems, coup_sems,
):
    n_row, n_col, nc, rows = sizes
    per = rows // LANES
    blocks = n_row * per
    tail = TAPS // LANES
    scale = 1.0 / (n_row * rows)
    my_row, my_col = lax.axis_index("row"), lax.axis_index("col")
    start = my_row * per
    turn = turn_matrix()
    zeros = jnp.zeros((1, TAPS), F32)
    read_lead(lead, seen, other, my_col, n_row, per)

    z = block_products(lead[8 : 8 + blocks, :], shifted(lead, blocks, -1, RIGHT), turn, LEFT)
    lags = skewed_sum(z)

    last = lead[8 + blocks - tail : 8 + blocks, :]
    expand(jnp.concatenate([in_row(last, range(tail)), zeros], 1), 0, TAPS, window, 0, 0)
    left = split(window[0:TAPS, :])
    tail_left = joined(left, LEFT[:SHORT], 1)
    expand(jnp.concatenate([in_row(flip(last, turn), reversed(range(tail))), zeros], 1), 1 + TAPS, TAPS, gram, 0, WIDE)
    extra = dot(joined(left, LEFT, 1), joined(split(gram[:, WIDE:]), RIGHT, 0))

    expand(lags, 1 + TAPS, WIDE, gram, 0, 0)
    gram[:, 0:WIDE] = (gram[:, 0:WIDE] + extra) * scale
    a = lax.broadcasted_iota(jnp.int32, (WIDE, WIDE), 0)
    b = lax.broadcasted_iota(jnp.int32, (WIDE, WIDE), 1)
    gram[:, WIDE:] = (a == b).astype(F32)

    for r in range(n_row):
        for q in range(per):
            t = r * per + q
            natural[t * nc : (t + 1) * nc, :] = seen[r, :, LANES * q : LANES * (q + 1)]
    rows_of = lambda t: natural[pl.ds(pl.multiple_of(t * nc, nc), nc), :]
    history = jnp.where(my_row > 0, 1.0, 0.0)
    near = [rows_of(jnp.maximum(start + q, 0)) * (history if q < 0 else 1.0) for q in range(-tail, per)]
    near += [rows_of(blocks - tail + q) for q in range(tail)]
    near = flip(jnp.concatenate(near, 0), turn)
    own = flip(lead[pl.ds(8 + start - tail, per + tail), :], turn)
    expand(in_row(own, reversed(range(per + tail))), 1 + TAPS, rows, window, 0, 0)
    own_rows = joined(split(window[0:rows, :], 2), LEFT[:SHORT], 1)
    right = shifted(lead, blocks, -tail, (0, 0, 1, 1))
    left = [joined(split(natural[pl.ds(c, blocks, stride=nc), :], 2), (0, 1), 0) for c in range(nc)]
    left = dot(turn, jnp.concatenate(left, 0), NT).astype(BF16)
    left = [left[:, 2 * blocks * c : 2 * blocks * (c + 1)] for c in range(nc)]
    left = jnp.concatenate([jnp.concatenate([x, x], 1) for x in left], 0)

    def steps():
        for u in range(0, right.shape[1], 2 * LANES):
            at = slice(u, min(u + 2 * LANES, right.shape[1]))
            products[:, at] = dot(left, right[:, at])
            yield
        for c in range(nc):
            last = [(per + tail + q) * nc + c for q in reversed(range(tail))]
            refs = (low_high.at[c], low_low.at[c])
            expand_split(jnp.concatenate([in_row(near, last), zeros], 1), 1 + TAPS, TAPS, refs)
            yield
        for c in range(nc):
            expand(skewed_sum(products[LANES * c : LANES * (c + 1), :]), 1 + TAPS, TAPS, cross, 0, c * TAPS)
            yield
        for c in range(nc):
            at = slice(c * TAPS, (c + 1) * TAPS)
            whole = cross[:, at] + dot(tail_left, joined((low_high[c], low_low[c]), RIGHT[:SHORT], 0))
            cross_high[c], cross_low[c] = split(whole * scale, 2)
            yield

    rest = steps()
    if FIRST:
        run(rest)
    inverse_factor(gram, WIDE, lambda n: [next(rest, None) for _ in range(n)])
    run(rest)

    pieces = split(gram[:, WIDE:], 2)
    factor = joined(pieces, LEFT[:SHORT], 1)
    panel = dot(own_rows, joined(pieces, RIGHT[:SHORT], 1), NT)
    basis = joined(split(panel, 2), LEFT[:SHORT], 1)
    copies = []

    def couple(c):
        at = slice(c * TAPS, (c + 1) * TAPS)
        coupling = dot(factor, joined((cross_high[c], cross_low[c]), RIGHT[:SHORT], 0))
        coup[:, at] = coupling
        copies.append(pltpu.make_async_copy(coup.at[:, at], coup_out.at[:, at], coup_sems.at[c]))
        copies[-1].start()
        expand(in_row(near, [q * nc + c for q in reversed(range(per + tail))]), 1 + TAPS, rows, over, 0, c * TAPS)
        return joined(split(coupling, 2), RIGHT[:SHORT], 0)

    ahead = couple(0)
    for c in range(nc):
        at = slice(c * TAPS, (c + 1) * TAPS)
        now = ahead
        if c + 1 < nc:
            ahead = couple(c + 1)
        rest = over[:, at] - dot(basis, now)
        if c * TAPS < WIDE:
            rest = jnp.where(my_col == 0, panel, rest)
        over[:, at] = rest
        copies.append(pltpu.make_async_copy(over.at[:, at], over_out.at[:, at], over_sems.at[c]))
        copies[-1].start()
    for copy in copies:
        copy.wait()


def call(sizes, other, seen):
    n_row, n_col, nc, rows = sizes
    blocks = n_row * rows // LANES
    return pl.pallas_call(
        functools.partial(kernel, sizes),
        out_shape=(
            jax.ShapeDtypeStruct((rows, nc * TAPS), F32),
            jax.ShapeDtypeStruct((WIDE, nc * TAPS), F32),
        ),
        in_specs=[pl.BlockSpec(memory_space=pltpu.VMEM)] * 2,
        out_specs=[pl.BlockSpec(memory_space=pl.ANY)] * 2,
        scratch_shapes=[
            pltpu.VMEM((blocks * nc, LANES), F32),
            pltpu.VMEM((blocks + 16, LANES), F32),
            pltpu.VMEM((WIDE, 2 * WIDE), F32),
            pltpu.VMEM((max(rows, TAPS), TAPS), F32),
            pltpu.VMEM((nc * LANES, 2 * TAPS + LANES), F32),
            pltpu.VMEM((nc, TAPS, TAPS), BF16),
            pltpu.VMEM((nc, TAPS, TAPS), BF16),
            pltpu.VMEM((WIDE, nc * TAPS), F32),
            pltpu.VMEM((nc, TAPS, TAPS), BF16),
            pltpu.VMEM((nc, TAPS, TAPS), BF16),
            pltpu.VMEM((rows, nc * TAPS), F32),
            pltpu.VMEM((WIDE, nc * TAPS), F32),
            pltpu.SemaphoreType.DMA((nc,)),
            pltpu.SemaphoreType.DMA((nc,)),
        ],
        compiler_params=pltpu.CompilerParams(vmem_limit_bytes=24 * 2**20),
    )(other, seen)


def body(traces):
    n_row, n_col = lax.axis_size("row"), lax.axis_size("col")
    nc, rows = traces.shape
    seen = lax.all_to_all(jnp.broadcast_to(traces[None], (n_row, nc, rows)), "row", 0, 0)
    col = lax.axis_index("col")
    first, step = seen[:, 0:1], 1
    while step < n_col:
        pairs = [(i, i ^ step) for i in range(n_col) if i ^ step < n_col]
        other = lax.ppermute(first, "col", pairs)
        first, step = jnp.where(col < step, first, other), 2 * step
    return call((n_row, n_col, nc, rows), other, seen)


def solution(mesh):
    return jax.shard_map(
        body,
        mesh=mesh,
        in_specs=(P("col", "row"),),
        out_specs=(P("row", "col"), P(None, "col")),
        check_vma=False,
    )
```
